512 devices in a mesh: tm: 128 (over z, y, core), head: 4 (over x).
Axes of the slice: x: 4, y: 4, z: 16, core: 2. Of those that a mesh axis runs over, the one named last changes fastest.
Arguments:
- queries: bfloat16 [128, 384, 24, 128], P('tm', None, 'head'), may hold values from -40 to 40
- key_vectors: bfloat16 [128, 384, 24, 128], P('tm', None, 'head'), may hold values from -40 to 40
- value_vectors: bfloat16 [128, 384, 24, 128], P('tm', None, 'head'), may hold values from -6 to 6
- head_class: int32 [24], replicated, may hold values from 0 to 1, as said below
- frame_mask: int32 [4, 4], replicated, may hold values from 0 to 1, as said below
Outputs:
- attended: bfloat16 [128, 384, 24, 128], P('tm', None, 'head')
The draws below stay inside these ranges and needn't reach their ends.
Inputs may be any that keep to these rules, and one draw needn't show every extreme that they name: `head_class`: head group g holds heads g * 6 to g * 6 + 5; each group holds 1 or 5 temporal heads, and groups 2k and 2k + 1 hold 6 temporal heads together. `frame_mask`: the diagonal is all ones.
All inputs are finite; a program needn't handle non-finite values.
Results may differ from the reference program's by a relative error of at most 0.0042.
Values may be sent and summed in bfloat16 or wider, within the bound.
A program may use at most 64 MiB of HBM per device.

```python
import jax
import jax.numpy as jnp
from jax import lax

HEADS = 24
HD = 128
PATCHES = 384
FB = 4
FRAMES = 128
HG = 6
LEAST_T = 1
MOST_T = 5
FBLK = 32


def shared_parts(key):
    shape = (FRAMES, PATCHES, HEADS, HD)
    base = jax.random.normal(key, shape, jnp.float32)
    patch_id = lax.broadcasted_iota(jnp.int32, shape, 1)
    head_id = lax.broadcasted_iota(jnp.int32, shape, 2)
    strength = 3.2 + 1.5 * ((patch_id // 16 + head_id) % 3).astype(jnp.float32)
    return base * strength


def draw_queries(key, part):
    aligned = shared_parts(key)
    key = jax.random.fold_in(key, 7)
    return jax.random.normal(key, aligned.shape, jnp.float32).astype(jnp.bfloat16)


def draw_key_vectors(key, part):
    aligned = shared_parts(key)
    key = jax.random.fold_in(key, 11)
    return jax.random.normal(key, aligned.shape, jnp.float32).astype(jnp.bfloat16)


def draw_head_class(key, part):
    key = jax.random.fold_in(key, 5)
    first_key, second_key = jax.random.split(key)
    pair_count = HEADS // HG // 2
    flipped = jax.random.randint(first_key, (pair_count,), 0, 2)
    is_heavy = jnp.stack([flipped, 1 - flipped], axis=1).reshape(-1)
    group_count = LEAST_T + is_heavy * (MOST_T - LEAST_T)
    ranking = jax.vmap(lambda one_key: jax.random.permutation(one_key, HG))(jax.random.split(second_key, 2 * pair_count))
    return (ranking < group_count[:, None]).astype(jnp.int32).reshape(-1)


def draw_frame_mask(key, part):
    key = jax.random.fold_in(key, 3)
    random_bits = jax.random.randint(key, (FB, FB), 0, 2)
    return jnp.maximum(random_bits, jnp.eye(FB, dtype=jnp.int32)).astype(jnp.int32)


def block_levels(key, shape, cuts, low, largest):
    loudness = 1.0
    for position, parts in cuts:
        draws = jax.random.uniform(jax.random.fold_in(jax.random.fold_in(key, 6), position), (parts,), jnp.float32, low / len(cuts), largest / len(cuts))
        loudness = loudness * jnp.repeat(jnp.exp(draws), shape[position] // parts).reshape((-1,) + (1,) * (len(shape) - 1 - position))
    return loudness


def noise(own_key, extent, scale, most, pieces=(), held_as=jnp.bfloat16):
    values = jax.random.normal(own_key, extent, jnp.float32) * scale
    if len(pieces) > 0:
        values = block_levels(own_key, extent, pieces, -0.22, 0.18) * values
    return jnp.clip(values, min=-most, max=most).astype(held_as)


def setup_inputs(seed: int = 0) -> dict:
    arg_keys = jax.random.split(jax.random.key(seed), 6)
    return {
        "queries": draw_queries(jax.random.fold_in(arg_keys[5], 71), 0),
        "key_vectors": draw_key_vectors(jax.random.fold_in(arg_keys[5], 71), 0),
        "value_vectors": noise(arg_keys[2], (FRAMES, PATCHES, HEADS, HD), 1.0, 6.0, ((0, 128), (2, 4))),
        "head_class": draw_head_class(jax.random.fold_in(arg_keys[5], 71), 0),
        "frame_mask": draw_frame_mask(jax.random.fold_in(arg_keys[5], 71), 0),
    }


def reference(queries, key_vectors, value_vectors, head_class, frame_mask):
    score_scale = HD ** -0.5
    sorted_heads = jnp.argsort(head_class, stable=True).astype(jnp.int32)
    head_rank = jnp.argsort(sorted_heads).astype(jnp.int32)
    half_heads = HEADS // 2
    spatial_heads = sorted_heads[:half_heads]
    temporal_heads = sorted_heads[half_heads:]

    def spatial_frame(triple):
        query_block, key_block, value_block = triple
        scores = jnp.einsum('ihd,jhd->hij', query_block.astype(jnp.float32), key_block.astype(jnp.float32)) * score_scale
        peak = jnp.max(scores, axis=-1, keepdims=True)
        exponent = jnp.exp(scores - peak)
        totals = jnp.sum(exponent, axis=-1)
        weights = lax.optimization_barrier(exponent.astype(jnp.bfloat16)).astype(jnp.float32)
        blended = jnp.einsum('hij,jhd->ihd', weights, value_block.astype(jnp.float32))
        return (blended / jnp.transpose(totals)[:, :, None]).astype(jnp.bfloat16)

    spatial_in = tuple(jnp.take(a, spatial_heads, axis=2) for a in (queries, key_vectors, value_vectors))
    spatial = lax.map(spatial_frame, spatial_in)

    frame_block = jnp.arange(FRAMES, dtype=jnp.int32) // FBLK
    allowed = frame_mask[frame_block][:, frame_block] == 1

    def temporal_position(triple):
        query_block, key_block, value_block = triple
        scores = jnp.einsum('fhd,ghd->hfg', query_block.astype(jnp.float32), key_block.astype(jnp.float32)) * score_scale
        scores = jnp.where(allowed[None], scores, jnp.float32(-1e30))
        peak = jnp.max(scores, axis=-1, keepdims=True)
        exponent = jnp.where(allowed[None], jnp.exp(scores - peak), jnp.float32(0.0))
        totals = jnp.sum(exponent, axis=-1)
        weights = lax.optimization_barrier(exponent.astype(jnp.bfloat16)).astype(jnp.float32)
        blended = jnp.einsum('hfg,ghd->fhd', weights, value_block.astype(jnp.float32))
        return (blended / jnp.transpose(totals)[:, :, None]).astype(jnp.bfloat16)

    temporal_in = tuple(jnp.swapaxes(jnp.take(a, temporal_heads, axis=2), 0, 1) for a in (queries, key_vectors, value_vectors))
    temporal = jnp.swapaxes(lax.map(temporal_position, temporal_in), 0, 1)
    combined = jnp.concatenate([spatial, temporal], axis=2)
    return jnp.take(combined, head_rank, axis=2)
```

```python
import functools

import jax
import jax.numpy as jnp
from jax import lax
from jax.experimental import pallas as pl
from jax.experimental.pallas import tpu as pltpu
from jax.sharding import PartitionSpec as P

MESH = pl.DeviceIdType.MESH
ROWS = 8
SLOTS = 3
SIDE = 8


def attend(query, key, value, scale, allowed=None):
    scores = (
        lax.dot_general(query, key, (((1,), (1,)), ((), ())), preferred_element_type=jnp.float32)
        * scale
    )
    if allowed is not None:
        scores = jnp.where(allowed, scores, jnp.float32(-1e30))
    peak = jnp.max(scores, axis=-1, keepdims=True)
    exponent = jnp.exp(scores - peak)
    if allowed is not None:
        exponent = jnp.where(allowed, exponent, jnp.float32(0.0))
    totals = jnp.sum(exponent, axis=-1, keepdims=True)
    blended = jnp.dot(exponent.astype(jnp.bfloat16), value, preferred_element_type=jnp.float32)
    return blended / totals


def worker_core(slot, y_rel):
    return jnp.where(
        slot == 0, 0, jnp.where(slot == 1, (y_rel != 0).astype(jnp.int32), (y_rel != 3).astype(jnp.int32))
    )


def z_step(count, n):
    half = (n + 1) // 2
    return jnp.where(lax.rem(n, 2) == 1, count // 2 - half, lax.rem(count // 2 + half, count))


def kernel(
    class_ref, mask_ref, q_hbm, k_hbm, v_hbm, out_ref,
    own, tsend, wsend, wrecv, rx, wide, blend, rsend, res, bsend,
    load_sem, wsend_sem, wrecv_sem, tsend_sem, trecv_sem, rsend_sem, rrecv_sem, bsend_sem, brecv_sem,
):
    me = lax.axis_index("tm")
    group = lax.axis_index("head")
    frames = rx.shape[1]
    heads = own.shape[1]
    tiles = own.shape[2]
    patches = tiles * ROWS
    depth = own.shape[-1]
    z_count = frames // SIDE
    per_z = tiles // z_count
    scale = depth ** (-0.5)
    z, y, core = me // SIDE, lax.rem(me // 2, 4), lax.rem(me, 2)
    partner = {"head": group + 1 - 2 * lax.rem(group, 2)}

    loads = [
        pltpu.make_async_copy(src, own.at[a], load_sem.at[a])
        for a, src in enumerate((q_hbm, k_hbm, v_hbm))
    ]
    for load in loads:
        load.start()

    barrier = pltpu.get_barrier_semaphore()
    pl.semaphore_signal(barrier, inc=1, device_id=partner, device_id_type=MESH)

    def greet(k, carry):
        pl.semaphore_signal(
            barrier, inc=1, device_id={"tm": lax.rem(me + k, frames)}, device_id_type=MESH
        )
        return carry

    lax.fori_loop(1, frames, greet, 0)

    classes = [class_ref[group * heads + h] for h in range(heads)]
    count = functools.reduce(lambda a, b: a + b, classes)
    heavy = count > heads // 2
    odd = jnp.int32(0)
    for h in range(heads):
        odd = odd + jnp.where(heavy, 1 - classes[h], classes[h]) * h

    def major(k):
        return k + (odd <= k).astype(jnp.int32)

    for load in loads:
        load.wait()

    first_t = jnp.where(heavy, major(0), odd)
    for a in range(3):
        tsend[0, :, a] = own[a, first_t]
    for s in range(SLOTS - 1):
        for a in range(3):
            wsend[s, a] = own[a, major(3 + s)]

    pl.semaphore_wait(barrier, frames)

    swaps = [
        pltpu.make_async_remote_copy(
            wsend.at[s], wrecv.at[s], wsend_sem.at[s], wrecv_sem.at[s],
            device_id=partner, device_id_type=MESH,
        )
        for s in range(SLOTS - 1)
    ]
    for swap in swaps:
        swap.start()

    def spread(slot):
        def body(n, carry):
            zz = lax.rem(z + z_step(z_count, n // per_z), z_count)
            i = lax.rem(n, per_z)
            y_rel = lax.rem(slot + 1 + i, 4)
            yy = lax.rem(zz + y_rel, 4)
            to = zz * SIDE + yy * 2 + worker_core(slot, y_rel)
            tile = zz * per_z + i
            src, dst = tsend.at[slot, tile], rx.at[slot // 2, me]

            @pl.when(to != me)
            def _():
                pltpu.make_async_remote_copy(
                    src, dst, tsend_sem.at[slot], trecv_sem.at[slot],
                    device_id={"tm": to}, device_id_type=MESH,
                ).start()

            @pl.when(to == me)
            def _():
                pltpu.make_async_copy(src, dst, trecv_sem.at[slot]).start()

            return carry

        lax.fori_loop(0, tiles, body, 0)

    def spatial(slot, triple):
        query, key, value = (x.reshape(patches, depth) for x in triple)
        step = 128
        for r in range(0, patches, step):
            part = attend(query[r : r + step], key, value, scale)
            res[SLOTS + slot, r // ROWS : (r + step) // ROWS] = part.reshape(
                step // ROWS, ROWS, depth
            ).astype(jnp.bfloat16)

    spread(0)
    for s in range(1, SLOTS):
        swaps[s - 1].wait_recv()
        for a in range(3):
            tsend[s, :, a] = jnp.where(heavy, own[a, major(s)], wrecv[s - 1, a])
        spread(s)

    first_s = jnp.where(heavy, odd, major(0))
    spatial(0, [own[a, first_s] for a in range(3)])
    for s in range(1, SLOTS):
        spatial(s, [jnp.where(heavy, wrecv[s - 1, a], own[a, major(s)]) for a in range(3)])

    block_total = mask_ref.shape[0]
    row_block = lax.broadcasted_iota(jnp.int32, (frames, frames), 0) // (frames // block_total)
    col_block = lax.broadcasted_iota(jnp.int32, (frames, frames), 1) // (frames // block_total)
    kept = jnp.zeros((frames, frames), jnp.int32)
    for r in range(block_total):
        for c in range(block_total):
            kept = jnp.where((row_block == r) & (col_block == c), mask_ref[r, c], kept)
    allowed = kept == 1

    y_mine = lax.rem(y - lax.rem(z, 4) + 4, 4)

    def role(slot):
        i = lax.rem(y_mine - slot + 3, 4)
        return i, (i < per_z) & (core == worker_core(slot, y_mine))

    def temporal(slot, carry):
        i, mine = role(slot)

        @pl.when(mine)
        def _():
            half = slot // 2
            pltpu.make_async_copy(rx.at[half], rx.at[half], trecv_sem.at[slot]).wait()
            for a in range(3):
                wide[a] = rx[half, :, a].astype(jnp.float32).reshape(frames * ROWS, depth)
            for p in range(ROWS):
                rows = pl.ds(p, frames, stride=ROWS)
                query, key, value = (wide[a, rows, :].astype(jnp.bfloat16) for a in range(3))
                blend[rows, :] = attend(query, key, value, scale, allowed)
            rsend[half] = blend[...].reshape(frames, ROWS, depth).astype(jnp.bfloat16)
            tile = z * per_z + i

            def body(n, c):
                to = lax.rem(z + z_step(z_count, n // SIDE), z_count) * SIDE + lax.rem(me + n, SIDE)
                src, dst = rsend.at[half, to], res.at[slot, tile]

                @pl.when(to != me)
                def _():
                    pltpu.make_async_remote_copy(
                        src, dst, rsend_sem.at[slot], rrecv_sem.at[slot],
                        device_id={"tm": to}, device_id_type=MESH,
                    ).start()

                @pl.when(to == me)
                def _():
                    pltpu.make_async_copy(src, dst, rrecv_sem.at[slot]).start()

                return c

            lax.fori_loop(0, frames, body, 0)

        return carry

    lax.fori_loop(0, SLOTS, temporal, 0)

    backs = []
    for s in range(1, SLOTS):
        pltpu.make_async_copy(res.at[s], res.at[s], rrecv_sem.at[s]).wait()
        bsend[s - 1] = jnp.where(heavy, res[SLOTS + s], res[s])
        back = pltpu.make_async_remote_copy(
            bsend.at[s - 1], res.at[2 * SLOTS - 1 + s], bsend_sem.at[s - 1], brecv_sem.at[s - 1],
            device_id=partner, device_id_type=MESH,
        )
        back.start()
        backs.append(back)

    pltpu.make_async_copy(res.at[0], res.at[0], rrecv_sem.at[0]).wait()

    for swap in swaps:
        swap.wait_send()
    for s in range(SLOTS):
        _, mine = role(s)

        @pl.when(mine)
        def _():
            most = tsend.at[s, pl.ds(0, tiles - 1)]
            pltpu.make_async_copy(most, most, tsend_sem.at[s]).wait()
            rest = rsend.at[s // 2, pl.ds(0, frames - 1)]
            pltpu.make_async_copy(rest, rest, rsend_sem.at[s]).wait()

        @pl.when(jnp.logical_not(mine))
        def _():
            pltpu.make_async_copy(tsend.at[s], tsend.at[s], tsend_sem.at[s]).wait()

    for back in backs:
        back.wait()

    for h in range(heads):
        k = h - (odd < h).astype(jnp.int32)
        from_major = jnp.where(k < SLOTS, jnp.where(heavy, k, SLOTS + k), SLOTS + k)
        from_odd = jnp.where(heavy, SLOTS, 0)
        out_ref[h] = res[jnp.where(odd == h, from_odd, from_major)]


def per_device(queries, key_vectors, value_vectors, head_class, frame_mask):
    _, patches, heads, depth = queries.shape
    frames = lax.axis_size("tm")
    tiles = patches // ROWS
    by_head = [
        jnp.transpose(a[0], (1, 0, 2)).reshape(heads, tiles, ROWS, depth)
        for a in (queries, key_vectors, value_vectors)
    ]
    bf16, f32 = jnp.bfloat16, jnp.float32
    tile = (ROWS, depth)
    dma = pltpu.SemaphoreType.DMA
    out = pl.pallas_call(
        kernel,
        out_shape=jax.ShapeDtypeStruct((heads, tiles, ROWS, depth), bf16),
        in_specs=[pl.BlockSpec(memory_space=pltpu.SMEM)] * 2 + [pl.BlockSpec(memory_space=pl.ANY)] * 3,
        out_specs=pl.BlockSpec(memory_space=pltpu.VMEM),
        scratch_shapes=[
            pltpu.VMEM((3, heads, tiles) + tile, bf16),
            pltpu.VMEM((SLOTS, tiles, 3) + tile, bf16),
            pltpu.VMEM((SLOTS - 1, 3, tiles) + tile, bf16),
            pltpu.VMEM((SLOTS - 1, 3, tiles) + tile, bf16),
            pltpu.VMEM((2, frames, 3) + tile, bf16),
            pltpu.VMEM((3, frames * ROWS, depth), f32),
            pltpu.VMEM((frames * ROWS, depth), f32),
            pltpu.VMEM((2, frames) + tile, bf16),
            pltpu.VMEM((3 * SLOTS - 1, tiles) + tile, bf16),
            pltpu.VMEM((SLOTS - 1, tiles) + tile, bf16),
            dma((3,)),
            dma((SLOTS - 1,)),
            dma((SLOTS - 1,)),
            dma((SLOTS,)),
            dma((SLOTS,)),
            dma((SLOTS,)),
            dma((SLOTS,)),
            dma((SLOTS - 1,)),
            dma((SLOTS - 1,)),
        ],
        compiler_params=pltpu.CompilerParams(
            collective_id=0, has_side_effects=True, vmem_limit_bytes=40 * 2**20
        ),
        name="split_heads_attention",
    )(head_class, frame_mask, *by_head)
    return jnp.transpose(out.reshape(heads, patches, depth), (1, 0, 2))[None]


def solution(mesh):
    spec = P("tm", None, "head", None)
    return jax.shard_map(
        per_device,
        mesh=mesh,
        in_specs=(spec, spec, spec, P(), P()),
        out_specs=spec,
        check_vma=False,
    )
```

```python
import functools

import jax
import jax.numpy as jnp
from jax import lax
from jax.experimental import pallas as pl
from jax.experimental.pallas import tpu as pltpu
from jax.sharding import PartitionSpec as P

MESH = pl.DeviceIdType.MESH
ROWS = 8
SLOTS = 3
SIDE = 8


def attend(query, key, value, scale, allowed=None):
    scores = (
        lax.dot_general(query, key, (((1,), (1,)), ((), ())), preferred_element_type=jnp.float32)
        * scale
    )
    if allowed is not None:
        scores = jnp.where(allowed, scores, jnp.float32(-1e30))
    peak = jnp.max(scores, axis=-1, keepdims=True)
    exponent = jnp.exp(scores - peak)
    if allowed is not None:
        exponent = jnp.where(allowed, exponent, jnp.float32(0.0))
    totals = jnp.sum(exponent, axis=-1, keepdims=True)
    blended = jnp.dot(exponent.astype(jnp.bfloat16), value, preferred_element_type=jnp.float32)
    return blended / totals


UNITS = ((0, 0), (0, 1), (1, 0), (1, 1), (1, 2), (2, 0), (2, 1), (2, 2), (0, 2))


def kernel(
    class_hbm, mask_hbm, q_hbm, k_hbm, v_hbm, out_ref,
    class_ref, mask_ref, own, tsend, wsend, wrecv, rx, wide, blend, rsend, res, bsend,
    load_sem, wsend_sem, wrecv_sem, tsend_sem, trecv_sem, rsend_sem, rrecv_sem, bsend_sem, brecv_sem,
):
    me = lax.axis_index("tm")
    group = lax.axis_index("head")
    frames = rx.shape[1]
    heads = own.shape[1]
    tiles = own.shape[2]
    patches = tiles * ROWS
    depth = own.shape[-1]
    z_count = frames // SIDE
    scale = depth ** (-0.5)
    z, y, core = me >> 3, (me >> 1) & 3, me & 1
    partner = {"head": group ^ 1}

    loads = [
        pltpu.make_async_copy(src, dst, load_sem.at[n])
        for n, (src, dst) in enumerate(
            (
                (class_hbm, class_ref),
                (q_hbm, own.at[0]),
                (k_hbm, own.at[1]),
                (v_hbm, own.at[2]),
                (mask_hbm, mask_ref),
            )
        )
    ]
    for load in loads:
        load.start()

    barrier = pltpu.get_barrier_semaphore()
    pl.semaphore_signal(barrier, inc=1, device_id=partner, device_id_type=MESH)

    def greet(n, carry):
        pl.semaphore_signal(
            barrier, inc=1, device_id={"tm": me ^ (frames - n)}, device_id_type=MESH
        )
        return carry

    lax.fori_loop(1, frames, greet, 0)

    for load in loads:
        load.wait()

    classes = [class_ref[group * heads + h] for h in range(heads)]
    count = functools.reduce(lambda a, b: a + b, classes)
    heavy = count > heads // 2
    odd = jnp.int32(0)
    for h in range(heads):
        odd = odd + jnp.where(heavy, 1 - classes[h], classes[h]) * h

    def major(k):
        return k + (odd <= k).astype(jnp.int32)

    def unit_rows(i):
        return pl.ds(i * z_count, z_count)

    def stage(unit):
        slot, i = UNITS[unit]
        for a in range(3):
            if slot == 0:
                block = own[a, jnp.where(heavy, major(0), odd), unit_rows(i)]
            else:
                block = jnp.where(heavy, own[a, major(slot), unit_rows(i)], wrecv[slot - 1, i, a])
            tsend[unit_rows(unit), a] = block

    def spatial(slot, triple):
        query, key, value = (x.reshape(patches, depth) for x in triple)
        step = 128
        for r in range(0, patches, step):
            part = attend(query[r : r + step], key, value, scale)
            res[SLOTS + slot, r // ROWS : (r + step) // ROWS] = part.reshape(
                step // ROWS, ROWS, depth
            ).astype(jnp.bfloat16)

    stage(0)
    for s in range(SLOTS - 1):
        for i in range(SLOTS):
            for a in range(3):
                wsend[s, i, a] = own[a, major(3 + s), unit_rows(i)]
    first_s = jnp.where(heavy, odd, major(0))
    spatial(0, [own[a, first_s] for a in range(3)])

    pl.semaphore_wait(barrier, frames)

    swaps = {
        (s, i): pltpu.make_async_remote_copy(
            wsend.at[s - 1, i], wrecv.at[s - 1, i], wsend_sem.at[s - 1, i], wrecv_sem.at[s - 1, i],
            device_id=partner, device_id_type=MESH,
        )
        for s in range(1, SLOTS)
        for i in range(SLOTS)
    }

    def spread(unit):
        half = 1 if unit == 1 else 0
        rank = max(unit - 1, 0)
        land, sem = rx.at[half, me], trecv_sem.at[half]
        first = unit * z_count

        def worker(zz):
            return zz * SIDE + ((zz + rank) & 3) * 2 + ((rank // 4 + (zz >> 2)) & 1)

        def send(zz):
            pltpu.make_async_remote_copy(
                tsend.at[first + zz], land, tsend_sem, sem,
                device_id={"tm": worker(zz)}, device_id_type=MESH,
            ).start()

        def body(n, carry):
            send(z ^ (z_count - n))
            return carry

        lax.fori_loop(1, z_count, body, 0)
        here = worker(z) == me

        @pl.when(here)
        def _():
            pltpu.make_async_copy(tsend.at[first + z], land, sem).start()

        @pl.when(jnp.logical_not(here))
        def _():
            send(z)

    block_total = mask_ref.shape[0]

    def temporal(unit, half):
        slot = jnp.where((unit < 2) | (unit == 8), 0, (unit + 1) // 3)
        i = jnp.where(unit < 2, unit, jnp.where(unit == 8, 2, lax.rem(unit + 1, 3)))
        row_block = lax.broadcasted_iota(jnp.int32, (frames, frames), 0) // (frames // block_total)
        col_block = lax.broadcasted_iota(jnp.int32, (frames, frames), 1) // (frames // block_total)
        kept = jnp.zeros((frames, frames), jnp.int32)
        for r in range(block_total):
            for c in range(block_total):
                kept = jnp.where((row_block == r) & (col_block == c), mask_ref[r, c], kept)
        allowed = kept == 1
        pltpu.make_async_copy(rx.at[half], rx.at[half], trecv_sem.at[half]).wait()
        for a in range(3):
            wide[a] = rx[half, :, a].astype(jnp.float32).reshape(frames * ROWS, depth)
        for p in range(ROWS):
            rows = pl.ds(p, frames, stride=ROWS)
            query, key, value = (wide[a, rows, :].astype(jnp.bfloat16) for a in range(3))
            blend[rows, :] = attend(query, key, value, scale, allowed)
        rsend[half] = blend[...].reshape(frames, ROWS, depth).astype(jnp.bfloat16)
        tile = i * z_count + z

        land, sem = res.at[slot, tile], rrecv_sem.at[slot]

        def body(n, carry):
            to = me ^ (frames - n)
            pltpu.make_async_remote_copy(
                rsend.at[half, to], land, rsend_sem.at[half], sem,
                device_id={"tm": to}, device_id_type=MESH,
            ).start()
            return carry

        lax.fori_loop(1, frames, body, 0)
        pltpu.make_async_copy(rsend.at[half, me], land, sem).start()

    my_rank = (core ^ ((z >> 2) & 1)) * 4 + ((y - z) & 3)
    twice = my_rank == 0

    for i in range(SLOTS):
        swaps[1, i].start()
    spread(0)
    stage(1)
    spread(1)
    for slot in range(1, SLOTS):
        for i in range(SLOTS):
            swaps[slot, i].wait_recv()
            if slot == 1:
                swaps[2, i].start()
            unit = UNITS.index((slot, i))
            stage(unit)
            spread(unit)
    stage(len(UNITS) - 1)
    spread(len(UNITS) - 1)

    for s in range(1, SLOTS):
        pieces = []
        for a in range(3):
            theirs = wrecv[s - 1, :, a].reshape(tiles, ROWS, depth)
            pieces.append(jnp.where(heavy, theirs, own[a, major(s)]))
        spatial(s, pieces)

    temporal(jnp.where(twice, 0, my_rank + 1), 0)

    def swap_back(s):
        pltpu.make_async_copy(res.at[s], res.at[s], rrecv_sem.at[s]).wait()
        bsend[s - 1] = jnp.where(heavy, res[SLOTS + s], res[s])
        back = pltpu.make_async_remote_copy(
            bsend.at[s - 1], res.at[2 * SLOTS - 1 + s], bsend_sem.at[s - 1], brecv_sem.at[s - 1],
            device_id=partner, device_id_type=MESH,
        )
        back.start()
        return back

    @pl.when(twice)
    def _():
        temporal(jnp.int32(1), 1)

    backs = [swap_back(1), swap_back(2)]
    pltpu.make_async_copy(res.at[0], res.at[0], rrecv_sem.at[0]).wait()

    for swap in swaps.values():
        swap.wait_send()

    def drain(buffer, sem):
        pltpu.make_async_copy(buffer, buffer, sem).wait()

    drain(rsend.at[0, pl.ds(0, frames - 1)], rsend_sem.at[0])

    @pl.when(twice)
    def _():
        drain(rsend.at[1, pl.ds(0, frames - 1)], rsend_sem.at[1])
        drain(tsend.at[pl.ds(0, len(UNITS) * z_count - 2)], tsend_sem)

    @pl.when(jnp.logical_not(twice))
    def _():
        drain(tsend.at[pl.ds(0, len(UNITS) * z_count - 1)], tsend_sem)

    for back in backs:
        back.wait()

    for h in range(heads):
        k = h - (odd < h).astype(jnp.int32)
        from_major = jnp.where(k < SLOTS, jnp.where(heavy, k, SLOTS + k), SLOTS + k)
        from_odd = jnp.where(heavy, SLOTS, 0)
        out_ref[h] = res[jnp.where(odd == h, from_odd, from_major)]


def per_device(queries, key_vectors, value_vectors, head_class, frame_mask):
    _, patches, heads, depth = queries.shape
    frames = lax.axis_size("tm")
    tiles = patches // ROWS
    by_head = [
        jnp.transpose(a[0], (1, 0, 2)).reshape(heads, tiles, ROWS, depth)
        for a in (queries, key_vectors, value_vectors)
    ]
    bf16, f32 = jnp.bfloat16, jnp.float32
    tile = (ROWS, depth)
    dma = pltpu.SemaphoreType.DMA
    out = pl.pallas_call(
        kernel,
        out_shape=jax.ShapeDtypeStruct((heads, tiles, ROWS, depth), bf16),
        in_specs=[pl.BlockSpec(memory_space=pltpu.HBM)] * 5,
        out_specs=pl.BlockSpec(memory_space=pltpu.VMEM),
        scratch_shapes=[
            pltpu.SMEM(head_class.shape, jnp.int32),
            pltpu.SMEM(frame_mask.shape, jnp.int32),
            pltpu.VMEM((3, heads, tiles) + tile, bf16),
            pltpu.VMEM((SLOTS * tiles, 3) + tile, bf16),
            pltpu.VMEM((SLOTS - 1, SLOTS, 3, tiles // SLOTS) + tile, bf16),
            pltpu.VMEM((SLOTS - 1, SLOTS, 3, tiles // SLOTS) + tile, bf16),
            pltpu.VMEM((2, frames, 3) + tile, bf16),
            pltpu.VMEM((3, frames * ROWS, depth), f32),
            pltpu.VMEM((frames * ROWS, depth), f32),
            pltpu.VMEM((2, frames) + tile, bf16),
            pltpu.VMEM((3 * SLOTS - 1, tiles) + tile, bf16),
            pltpu.VMEM((SLOTS - 1, tiles) + tile, bf16),
            dma((5,)),
            dma((SLOTS - 1, SLOTS)),
            dma((SLOTS - 1, SLOTS)),
            dma,
            dma((2,)),
            dma((2,)),
            dma((SLOTS,)),
            dma((SLOTS - 1,)),
            dma((SLOTS - 1,)),
        ],
        compiler_params=pltpu.CompilerParams(
            collective_id=0, has_side_effects=True, vmem_limit_bytes=40 * 2**20
        ),
        name="split_heads_attention",
    )(head_class, frame_mask, *by_head)
    return jnp.transpose(out.reshape(heads, patches, depth), (1, 0, 2))[None]


def solution(mesh):
    spec = P("tm", None, "head", None)
    return jax.shard_map(
        per_device,
        mesh=mesh,
        in_specs=(spec, spec, spec, P(), P()),
        out_specs=spec,
        check_vma=False,
    )
```

```python
import functools

import jax
import jax.numpy as jnp
from jax import lax
from jax.experimental import pallas as pl
from jax.experimental.pallas import tpu as pltpu
from jax.sharding import PartitionSpec as P

MESH = pl.DeviceIdType.MESH
ROWS = 8
SLOTS = 3
SIDE = 8


def attend(query, key, value, scale, allowed=None):
    scores = (
        lax.dot_general(query, key, (((1,), (1,)), ((), ())), preferred_element_type=jnp.float32)
        * scale
    )
    if allowed is not None:
        scores = jnp.where(allowed, scores, jnp.float32(-1e30))
    peak = jnp.max(scores, axis=-1, keepdims=True)
    exponent = jnp.exp(scores - peak)
    if allowed is not None:
        exponent = jnp.where(allowed, exponent, jnp.float32(0.0))
    totals = jnp.sum(exponent, axis=-1, keepdims=True)
    blended = jnp.dot(exponent.astype(jnp.bfloat16), value, preferred_element_type=jnp.float32)
    return blended / totals


UNITS = ((0, 0), (0, 1), (1, 0), (1, 1), (1, 2), (2, 0), (2, 1), (2, 2), (0, 2))


def kernel(
    class_hbm, mask_hbm, q_hbm, k_hbm, v_hbm, out_ref,
    class_ref, mask_ref, own, tsend, wsend, wrecv, rx, wide, blend, rsend, res, bsend,
    load_sem, wsend_sem, wrecv_sem, tsend_sem, trecv_sem, rsend_sem, rrecv_sem, bsend_sem, brecv_sem,
):
    me = lax.axis_index("tm")
    group = lax.axis_index("head")
    frames = rx.shape[1]
    heads = own.shape[1]
    tiles = own.shape[2]
    patches = tiles * ROWS
    depth = own.shape[-1]
    z_count = frames // SIDE
    scale = depth ** (-0.5)
    z, y, core = me >> 3, (me >> 1) & 3, me & 1
    partner = {"head": group ^ 1}

    loads = [
        pltpu.make_async_copy(src, dst, load_sem.at[n])
        for n, (src, dst) in enumerate(
            (
                (class_hbm, class_ref),
                (q_hbm, own.at[0]),
                (k_hbm, own.at[1]),
                (v_hbm, own.at[2]),
                (mask_hbm, mask_ref),
            )
        )
    ]
    for load in loads:
        load.start()

    barrier = pltpu.get_barrier_semaphore()
    pl.semaphore_signal(barrier, inc=1, device_id=partner, device_id_type=MESH)

    def step_z(n):
        step = n * 7
        return (z + jnp.where(core == 0, step, -step)) & (z_count - 1)

    def greet(n, carry):
        pl.semaphore_signal(
            barrier, inc=1, device_id={"tm": me ^ (frames - n)}, device_id_type=MESH
        )
        return carry

    lax.fori_loop(1, frames, greet, 0)

    for load in loads:
        load.wait()

    classes = [class_ref[group * heads + h] for h in range(heads)]
    count = functools.reduce(lambda a, b: a + b, classes)
    heavy = count > heads // 2
    odd = jnp.int32(0)
    for h in range(heads):
        odd = odd + jnp.where(heavy, 1 - classes[h], classes[h]) * h

    def major(k):
        return k + (odd <= k).astype(jnp.int32)

    def unit_rows(i):
        return pl.ds(i * z_count, z_count)

    def stage(unit):
        slot, i = UNITS[unit]
        for a in range(3):
            if slot == 0:
                block = own[a, jnp.where(heavy, major(0), odd), unit_rows(i)]
            else:
                block = jnp.where(heavy, own[a, major(slot), unit_rows(i)], wrecv[slot - 1, i, a])
            tsend[unit_rows(unit), a] = block

    def spatial(slot, triple):
        query, key, value = (x.reshape(patches, depth) for x in triple)
        step = 128
        for r in range(0, patches, step):
            part = attend(query[r : r + step], key, value, scale)
            res[SLOTS + slot, r // ROWS : (r + step) // ROWS] = part.reshape(
                step // ROWS, ROWS, depth
            ).astype(jnp.bfloat16)

    stage(0)
    for s in range(SLOTS - 1):
        for i in range(SLOTS):
            for a in range(3):
                wsend[s, i, a] = own[a, major(3 + s), unit_rows(i)]
    first_s = jnp.where(heavy, odd, major(0))
    spatial(0, [own[a, first_s] for a in range(3)])

    pl.semaphore_wait(barrier, frames)

    swaps = {
        (s, i): pltpu.make_async_remote_copy(
            wsend.at[s - 1, i], wrecv.at[s - 1, i], wsend_sem.at[s - 1, i], wrecv_sem.at[s - 1, i],
            device_id=partner, device_id_type=MESH,
        )
        for s in range(1, SLOTS)
        for i in range(SLOTS)
    }

    def spread(unit):
        half = 1 if unit == 1 else 0
        rank = max(unit - 1, 0)
        land, sem = rx.at[half, me], trecv_sem.at[half]
        first = unit * z_count

        def worker(zz):
            return zz * SIDE + ((zz + rank) & 3) * 2 + ((rank // 4 + (zz >> 2)) & 1)

        def send(zz):
            pltpu.make_async_remote_copy(
                tsend.at[first + zz], land, tsend_sem, sem,
                device_id={"tm": worker(zz)}, device_id_type=MESH,
            ).start()

        def body(n, carry):
            send(step_z(n))
            return carry

        lax.fori_loop(1, z_count, body, 0)
        here = worker(z) == me

        @pl.when(here)
        def _():
            pltpu.make_async_copy(tsend.at[first + z], land, sem).start()

        @pl.when(jnp.logical_not(here))
        def _():
            send(z)

    block_total = mask_ref.shape[0]

    def temporal(unit, half):
        slot = jnp.where((unit < 2) | (unit == 8), 0, (unit + 1) // 3)
        i = jnp.where(unit < 2, unit, jnp.where(unit == 8, 2, lax.rem(unit + 1, 3)))
        row_block = lax.broadcasted_iota(jnp.int32, (frames, frames), 0) // (frames // block_total)
        col_block = lax.broadcasted_iota(jnp.int32, (frames, frames), 1) // (frames // block_total)
        kept = jnp.zeros((frames, frames), jnp.int32)
        for r in range(block_total):
            for c in range(block_total):
                kept = jnp.where((row_block == r) & (col_block == c), mask_ref[r, c], kept)
        allowed = kept == 1
        pltpu.make_async_copy(rx.at[half], rx.at[half], trecv_sem.at[half]).wait()
        for a in range(3):
            wide[a] = rx[half, :, a].astype(jnp.float32).reshape(frames * ROWS, depth)
        for p in range(ROWS):
            rows = pl.ds(p, frames, stride=ROWS)
            query, key, value = (wide[a, rows, :].astype(jnp.bfloat16) for a in range(3))
            blend[rows, :] = attend(query, key, value, scale, allowed)
        rsend[half] = blend[...].reshape(frames, ROWS, depth).astype(jnp.bfloat16)
        tile = i * z_count + z

        land, sem = res.at[slot, tile], rrecv_sem.at[unit]

        def give(to):
            @pl.when(to != me)
            def _():
                pltpu.make_async_remote_copy(
                    rsend.at[half, to], land, rsend_sem.at[half], sem,
                    device_id={"tm": to}, device_id_type=MESH,
                ).start()

        def body(n, carry):
            zz, turn = step_z(n), n >> 4
            early = zz < 2
            late = zz >= 8
            one = jnp.where(early, 2 * turn, jnp.where(late, jnp.where(turn < 6, turn - 2, 2 * turn - SIDE), turn))
            two = (early & (turn < 4)) | (late & (turn >= 6))

            @pl.when((one >= 0) & (one < SIDE))
            def _():
                give(zz * SIDE + ((me ^ one) & (SIDE - 1)))

            @pl.when(two)
            def _():
                give(zz * SIDE + ((me ^ (one + 1)) & (SIDE - 1)))

            return carry

        lax.fori_loop(0, frames, body, 0)
        pltpu.make_async_copy(rsend.at[half, me], land, sem).start()

    my_rank = (core ^ ((z >> 2) & 1)) * 4 + ((y - z) & 3)
    twice = my_rank == 0

    for i in range(SLOTS):
        swaps[1, i].start()
    spread(0)
    stage(1)
    spread(1)
    for slot in range(1, SLOTS):
        for i in range(SLOTS):
            swaps[slot, i].wait_recv()
            if slot == 1:
                swaps[2, i].start()
            unit = UNITS.index((slot, i))
            stage(unit)
            spread(unit)
    stage(len(UNITS) - 1)
    spread(len(UNITS) - 1)

    for s in range(1, SLOTS):
        pieces = []
        for a in range(3):
            theirs = wrecv[s - 1, :, a].reshape(tiles, ROWS, depth)
            pieces.append(jnp.where(heavy, theirs, own[a, major(s)]))
        spatial(s, pieces)

    temporal(jnp.where(twice, 0, my_rank + 1), 0)

    @pl.when(twice)
    def _():
        temporal(jnp.int32(1), 1)

    def landed(unit):
        slot, i = UNITS[unit]
        part = res.at[slot, unit_rows(i)]
        pltpu.make_async_copy(part, part, rrecv_sem.at[unit]).wait()

    backs = []
    for unit, (slot, i) in enumerate(UNITS):
        if slot > 0:
            landed(unit)
            rows = unit_rows(i)
            bsend[slot - 1, rows] = jnp.where(heavy, res[SLOTS + slot, rows], res[slot, rows])
            back = pltpu.make_async_remote_copy(
                bsend.at[slot - 1, rows], res.at[2 * SLOTS - 1 + slot, rows],
                bsend_sem.at[slot - 1, i], brecv_sem.at[slot - 1, i],
                device_id=partner, device_id_type=MESH,
            )
            back.start()
            backs.append(back)

    for unit, (slot, _) in enumerate(UNITS):
        if slot == 0:
            landed(unit)

    for swap in swaps.values():
        swap.wait_send()

    def drain(buffer, sem):
        pltpu.make_async_copy(buffer, buffer, sem).wait()

    drain(rsend.at[0, pl.ds(0, frames - 1)], rsend_sem.at[0])

    @pl.when(twice)
    def _():
        drain(rsend.at[1, pl.ds(0, frames - 1)], rsend_sem.at[1])
        drain(tsend.at[pl.ds(0, len(UNITS) * z_count - 2)], tsend_sem)

    @pl.when(jnp.logical_not(twice))
    def _():
        drain(tsend.at[pl.ds(0, len(UNITS) * z_count - 1)], tsend_sem)

    for back in backs:
        back.wait()

    for h in range(heads):
        k = h - (odd < h).astype(jnp.int32)
        from_major = jnp.where(k < SLOTS, jnp.where(heavy, k, SLOTS + k), SLOTS + k)
        from_odd = jnp.where(heavy, SLOTS, 0)
        out_ref[h] = res[jnp.where(odd == h, from_odd, from_major)]


def per_device(queries, key_vectors, value_vectors, head_class, frame_mask):
    _, patches, heads, depth = queries.shape
    frames = lax.axis_size("tm")
    tiles = patches // ROWS
    by_head = [
        jnp.transpose(a[0], (1, 0, 2)).reshape(heads, tiles, ROWS, depth)
        for a in (queries, key_vectors, value_vectors)
    ]
    bf16, f32 = jnp.bfloat16, jnp.float32
    tile = (ROWS, depth)
    dma = pltpu.SemaphoreType.DMA
    out = pl.pallas_call(
        kernel,
        out_shape=jax.ShapeDtypeStruct((heads, tiles, ROWS, depth), bf16),
        in_specs=[pl.BlockSpec(memory_space=pltpu.HBM)] * 5,
        out_specs=pl.BlockSpec(memory_space=pltpu.VMEM),
        scratch_shapes=[
            pltpu.SMEM(head_class.shape, jnp.int32),
            pltpu.SMEM(frame_mask.shape, jnp.int32),
            pltpu.VMEM((3, heads, tiles) + tile, bf16),
            pltpu.VMEM((SLOTS * tiles, 3) + tile, bf16),
            pltpu.VMEM((SLOTS - 1, SLOTS, 3, tiles // SLOTS) + tile, bf16),
            pltpu.VMEM((SLOTS - 1, SLOTS, 3, tiles // SLOTS) + tile, bf16),
            pltpu.VMEM((2, frames, 3) + tile, bf16),
            pltpu.VMEM((3, frames * ROWS, depth), f32),
            pltpu.VMEM((frames * ROWS, depth), f32),
            pltpu.VMEM((2, frames) + tile, bf16),
            pltpu.VMEM((3 * SLOTS - 1, tiles) + tile, bf16),
            pltpu.VMEM((SLOTS - 1, tiles) + tile, bf16),
            dma((5,)),
            dma((SLOTS - 1, SLOTS)),
            dma((SLOTS - 1, SLOTS)),
            dma,
            dma((2,)),
            dma((2,)),
            dma((len(UNITS),)),
            dma((SLOTS - 1, SLOTS)),
            dma((SLOTS - 1, SLOTS)),
        ],
        compiler_params=pltpu.CompilerParams(
            collective_id=0, has_side_effects=True, vmem_limit_bytes=40 * 2**20
        ),
        name="split_heads_attention",
    )(head_class, frame_mask, *by_head)
    return jnp.transpose(out.reshape(heads, patches, depth), (1, 0, 2))[None]


def solution(mesh):
    spec = P("tm", None, "head", None)
    return jax.shard_map(
        per_device,
        mesh=mesh,
        in_specs=(spec, spec, spec, P(), P()),
        out_specs=spec,
        check_vma=False,
    )
```

```python
import functools

import jax
import jax.numpy as jnp
from jax import lax
from jax.experimental import pallas as pl
from jax.experimental.pallas import tpu as pltpu
from jax.sharding import PartitionSpec as P

MESH = pl.DeviceIdType.MESH
ROWS = 8
SLOTS = 3
SIDE = 8


def attend(query, key, value, scale, allowed=None):
    scores = (
        lax.dot_general(query, key, (((1,), (1,)), ((), ())), preferred_element_type=jnp.float32)
        * scale
    )
    if allowed is not None:
        scores = jnp.where(allowed, scores, jnp.float32(-1e30))
    peak = jnp.max(scores, axis=-1, keepdims=True)
    exponent = jnp.exp(scores - peak)
    if allowed is not None:
        exponent = jnp.where(allowed, exponent, jnp.float32(0.0))
    totals = jnp.sum(exponent, axis=-1, keepdims=True)
    blended = jnp.dot(exponent.astype(jnp.bfloat16), value, preferred_element_type=jnp.float32)
    return blended / totals


UNITS = ((0, 0), (0, 1), (1, 0), (1, 1), (1, 2), (2, 0), (2, 1), (2, 2), (0, 2))


def kernel(
    class_hbm, mask_hbm, q_hbm, k_hbm, v_hbm, out_ref,
    class_ref, mask_ref, own, tsend, wsend, wrecv, rx, wide, blend, rsend, res, bsend,
    load_sem, wsend_sem, wrecv_sem, tsend_sem, trecv_sem, rsend_sem, rrecv_sem, bsend_sem, brecv_sem,
):
    me = lax.axis_index("tm")
    group = lax.axis_index("head")
    frames = rx.shape[1]
    heads = own.shape[1]
    tiles = own.shape[2]
    patches = tiles * ROWS
    depth = own.shape[-1]
    z_count = frames // SIDE
    scale = depth ** (-0.5)
    z, y, core = me >> 3, (me >> 1) & 3, me & 1
    partner = {"head": group ^ 1}

    loads = [
        pltpu.make_async_copy(src, dst, load_sem.at[n])
        for n, (src, dst) in enumerate(
            (
                (class_hbm, class_ref),
                (q_hbm, own.at[0]),
                (k_hbm, own.at[1]),
                (v_hbm, own.at[2]),
                (mask_hbm, mask_ref),
            )
        )
    ]
    for load in loads:
        load.start()

    barrier = pltpu.get_barrier_semaphore()
    pl.semaphore_signal(barrier, inc=1, device_id=partner, device_id_type=MESH)

    def step_z(n):
        step = n * 7
        return (z + jnp.where(core == 0, step, -step)) & (z_count - 1)

    def greet(n, carry):
        turn = n >> 3
        half = (turn + 1) >> 1
        zz = (z + z_count // 2 + jnp.where((turn & 1) == 1, -half, half)) & (z_count - 1)
        pl.semaphore_signal(
            barrier,
            inc=1,
            device_id={"tm": zz * SIDE + ((me ^ (SIDE - 1 - (n & (SIDE - 1)))) & (SIDE - 1))},
            device_id_type=MESH,
        )
        return carry

    lax.fori_loop(0, frames - 1, greet, 0)

    for load in loads:
        load.wait()

    classes = [class_ref[group * heads + h] for h in range(heads)]
    count = functools.reduce(lambda a, b: a + b, classes)
    heavy = count > heads // 2
    odd = jnp.int32(0)
    for h in range(heads):
        odd = odd + jnp.where(heavy, 1 - classes[h], classes[h]) * h

    def major(k):
        return k + (odd <= k).astype(jnp.int32)

    def unit_rows(i):
        return pl.ds(i * z_count, z_count)

    def stage(unit):
        slot, i = UNITS[unit]
        for a in range(3):
            if slot == 0:
                block = own[a, jnp.where(heavy, major(0), odd), unit_rows(i)]
            else:
                block = jnp.where(heavy, own[a, major(slot), unit_rows(i)], wrecv[slot - 1, i, a])
            tsend[unit_rows(unit), a] = block

    def spatial(slot, triple):
        query, key, value = (x.reshape(patches, depth) for x in triple)
        step = 128
        for r in range(0, patches, step):
            part = attend(query[r : r + step], key, value, scale)
            res[SLOTS + slot, r // ROWS : (r + step) // ROWS] = part.reshape(
                step // ROWS, ROWS, depth
            ).astype(jnp.bfloat16)

    stage(0)
    for s in range(SLOTS - 1):
        for i in range(SLOTS):
            for a in range(3):
                wsend[s, i, a] = own[a, major(3 + s), unit_rows(i)]
    first_s = jnp.where(heavy, odd, major(0))
    spatial(0, [own[a, first_s] for a in range(3)])

    pl.semaphore_wait(barrier, frames)

    swaps = {
        (s, i): pltpu.make_async_remote_copy(
            wsend.at[s - 1, i], wrecv.at[s - 1, i], wsend_sem.at[s - 1, i], wrecv_sem.at[s - 1, i],
            device_id=partner, device_id_type=MESH,
        )
        for s in range(1, SLOTS)
        for i in range(SLOTS)
    }

    def spread(unit):
        half = 1 if unit == 1 else 0
        rank = max(unit - 1, 0)
        land, sem = rx.at[half, me], trecv_sem.at[half]
        first = unit * z_count

        def worker(zz):
            return zz * SIDE + ((zz + rank) & 3) * 2 + ((rank // 4 + (zz >> 2)) & 1)

        def send(zz):
            pltpu.make_async_remote_copy(
                tsend.at[first + zz], land, tsend_sem, sem,
                device_id={"tm": worker(zz)}, device_id_type=MESH,
            ).start()

        def body(n, carry):
            send(step_z(n))
            return carry

        lax.fori_loop(1, z_count, body, 0)
        here = worker(z) == me

        @pl.when(here)
        def _():
            pltpu.make_async_copy(tsend.at[first + z], land, sem).start()

        @pl.when(jnp.logical_not(here))
        def _():
            send(z)

    block_total = mask_ref.shape[0]

    def temporal(unit, half):
        slot = jnp.where((unit < 2) | (unit == 8), 0, (unit + 1) // 3)
        i = jnp.where(unit < 2, unit, jnp.where(unit == 8, 2, lax.rem(unit + 1, 3)))
        row_block = lax.broadcasted_iota(jnp.int32, (frames, frames), 0) // (frames // block_total)
        col_block = lax.broadcasted_iota(jnp.int32, (frames, frames), 1) // (frames // block_total)
        kept = jnp.zeros((frames, frames), jnp.int32)
        for r in range(block_total):
            for c in range(block_total):
                kept = jnp.where((row_block == r) & (col_block == c), mask_ref[r, c], kept)
        allowed = kept == 1
        pltpu.make_async_copy(rx.at[half], rx.at[half], trecv_sem.at[half]).wait()
        for a in range(3):
            wide[a] = rx[half, :, a].astype(jnp.float32).reshape(frames * ROWS, depth)
        for p in range(ROWS):
            rows = pl.ds(p, frames, stride=ROWS)
            query, key, value = (wide[a, rows, :].astype(jnp.bfloat16) for a in range(3))
            blend[rows, :] = attend(query, key, value, scale, allowed)
        rsend[half] = blend[...].reshape(frames, ROWS, depth).astype(jnp.bfloat16)
        tile = i * z_count + z

        land, sem = res.at[slot, tile], rrecv_sem.at[unit]

        def give(to):
            @pl.when(to != me)
            def _():
                pltpu.make_async_remote_copy(
                    rsend.at[half, to], land, rsend_sem.at[half], sem,
                    device_id={"tm": to}, device_id_type=MESH,
                ).start()

        def body(n, carry):
            zz, turn = step_z(n), n >> 4
            early = zz < 2
            late = zz >= 8
            one = jnp.where(early, 2 * turn, jnp.where(late, jnp.where(turn < 6, turn - 2, 2 * turn - SIDE), turn))
            two = (early & (turn < 4)) | (late & (turn >= 6))

            @pl.when((one >= 0) & (one < SIDE))
            def _():
                give(zz * SIDE + ((me ^ one) & (SIDE - 1)))

            @pl.when(two)
            def _():
                give(zz * SIDE + ((me ^ (one + 1)) & (SIDE - 1)))

            return carry

        lax.fori_loop(0, frames, body, 0)
        pltpu.make_async_copy(rsend.at[half, me], land, sem).start()

    my_rank = (core ^ ((z >> 2) & 1)) * 4 + ((y - z) & 3)
    twice = my_rank == 0

    for i in range(SLOTS):
        swaps[1, i].start()
    spread(0)
    stage(1)
    spread(1)
    for slot in range(1, SLOTS):
        for i in range(SLOTS):
            swaps[slot, i].wait_recv()
            if slot == 1:
                swaps[2, i].start()
            unit = UNITS.index((slot, i))
            stage(unit)
            spread(unit)
    stage(len(UNITS) - 1)
    spread(len(UNITS) - 1)

    for s in range(1, SLOTS):
        pieces = []
        for a in range(3):
            theirs = wrecv[s - 1, :, a].reshape(tiles, ROWS, depth)
            pieces.append(jnp.where(heavy, theirs, own[a, major(s)]))
        spatial(s, pieces)

    temporal(jnp.where(twice, 0, my_rank + 1), 0)

    @pl.when(twice)
    def _():
        temporal(jnp.int32(1), 1)

    def landed(unit):
        slot, i = UNITS[unit]
        part = res.at[slot, unit_rows(i)]
        pltpu.make_async_copy(part, part, rrecv_sem.at[unit]).wait()

    backs = []
    for unit, (slot, i) in enumerate(UNITS):
        if slot > 0:
            landed(unit)
            rows = unit_rows(i)
            bsend[slot - 1, rows] = jnp.where(heavy, res[SLOTS + slot, rows], res[slot, rows])
            back = pltpu.make_async_remote_copy(
                bsend.at[slot - 1, rows], res.at[2 * SLOTS - 1 + slot, rows],
                bsend_sem.at[slot - 1, i], brecv_sem.at[slot - 1, i],
                device_id=partner, device_id_type=MESH,
            )
            back.start()
            backs.append(back)

    for unit, (slot, _) in enumerate(UNITS):
        if slot == 0:
            landed(unit)

    for swap in swaps.values():
        swap.wait_send()

    def drain(buffer, sem):
        pltpu.make_async_copy(buffer, buffer, sem).wait()

    drain(rsend.at[0, pl.ds(0, frames - 1)], rsend_sem.at[0])

    @pl.when(twice)
    def _():
        drain(rsend.at[1, pl.ds(0, frames - 1)], rsend_sem.at[1])
        drain(tsend.at[pl.ds(0, len(UNITS) * z_count - 2)], tsend_sem)

    @pl.when(jnp.logical_not(twice))
    def _():
        drain(tsend.at[pl.ds(0, len(UNITS) * z_count - 1)], tsend_sem)

    for back in backs:
        back.wait()

    for h in range(heads):
        k = h - (odd < h).astype(jnp.int32)
        from_major = jnp.where(k < SLOTS, jnp.where(heavy, k, SLOTS + k), SLOTS + k)
        from_odd = jnp.where(heavy, SLOTS, 0)
        out_ref[h] = res[jnp.where(odd == h, from_odd, from_major)]


def per_device(queries, key_vectors, value_vectors, head_class, frame_mask):
    _, patches, heads, depth = queries.shape
    frames = lax.axis_size("tm")
    tiles = patches // ROWS
    by_head = [
        jnp.transpose(a[0], (1, 0, 2)).reshape(heads, tiles, ROWS, depth)
        for a in (queries, key_vectors, value_vectors)
    ]
    bf16, f32 = jnp.bfloat16, jnp.float32
    tile = (ROWS, depth)
    dma = pltpu.SemaphoreType.DMA
    out = pl.pallas_call(
        kernel,
        out_shape=jax.ShapeDtypeStruct((heads, tiles, ROWS, depth), bf16),
        in_specs=[pl.BlockSpec(memory_space=pltpu.HBM)] * 5,
        out_specs=pl.BlockSpec(memory_space=pltpu.VMEM),
        scratch_shapes=[
            pltpu.SMEM(head_class.shape, jnp.int32),
            pltpu.SMEM(frame_mask.shape, jnp.int32),
            pltpu.VMEM((3, heads, tiles) + tile, bf16),
            pltpu.VMEM((SLOTS * tiles, 3) + tile, bf16),
            pltpu.VMEM((SLOTS - 1, SLOTS, 3, tiles // SLOTS) + tile, bf16),
            pltpu.VMEM((SLOTS - 1, SLOTS, 3, tiles // SLOTS) + tile, bf16),
            pltpu.VMEM((2, frames, 3) + tile, bf16),
            pltpu.VMEM((3, frames * ROWS, depth), f32),
            pltpu.VMEM((frames * ROWS, depth), f32),
            pltpu.VMEM((2, frames) + tile, bf16),
            pltpu.VMEM((3 * SLOTS - 1, tiles) + tile, bf16),
            pltpu.VMEM((SLOTS - 1, tiles) + tile, bf16),
            dma((5,)),
            dma((SLOTS - 1, SLOTS)),
            dma((SLOTS - 1, SLOTS)),
            dma,
            dma((2,)),
            dma((2,)),
            dma((len(UNITS),)),
            dma((SLOTS - 1, SLOTS)),
            dma((SLOTS - 1, SLOTS)),
        ],
        compiler_params=pltpu.CompilerParams(
            collective_id=0, has_side_effects=True, vmem_limit_bytes=40 * 2**20
        ),
        name="split_heads_attention",
    )(head_class, frame_mask, *by_head)
    return jnp.transpose(out.reshape(heads, patches, depth), (1, 0, 2))[None]


def solution(mesh):
    spec = P("tm", None, "head", None)
    return jax.shard_map(
        per_device,
        mesh=mesh,
        in_specs=(spec, spec, spec, P(), P()),
        out_specs=spec,
        check_vma=False,
    )
```
